512 devices in a mesh: member: 16 (over x, y_hi, core), tile: 32 (over z, y_lo).
Axes of the slice: x: 4, y: 8 (y_hi: 2, y_lo: 4; y = y_hi * 4 + y_lo), z: 8, core: 2. Of those that a mesh axis runs over, the one named last changes fastest.
Arguments:
- ensemble: float32 [16, 3, 8, 512, 768], P('member', None, None, 'tile'), may hold values from -6 to 6
- winds: float32 [2, 8, 512, 768], P(None, None, 'tile'), may hold values from -0.35 to 0.35
- diffusion: float32 [8], replicated, may hold values from 0.01 to 0.07
- labels: int32 [512, 768], P('tile'), may hold values from 0 to 15, as said below
- amplitude: float32 [16], replicated, may hold values from 0.5 to 2
Outputs:
- bred: float32 [16, 3, 8, 512, 768], P('member', None, None, 'tile')
The draws below stay inside these ranges and needn't reach their ends.
Inputs may be any that keep to these rules, and one draw needn't show every extreme that they name: Every region labels at least one column.
All inputs are finite; a program needn't handle non-finite values.
Results may differ from the reference program's by a relative error of at most 0.00017.
Values sent between devices are 32-bit elements; how exact they have to be, the bound alone decides.
A program may use at most 64 MiB of HBM per device.

```python
import math
import jax
import jax.numpy as jnp
from jax import lax

CY = 768
LEVELS = 8
FIELDS = 3
REGIONS = 16
MEMBERS = 16
NX = 512


def draw_labels(key, part):
    key = jax.random.fold_in(key, 11)
    drawn = jax.random.randint(key, (NX, CY), 0, REGIONS, dtype=jnp.int32)
    return drawn.at[0, :REGIONS].set(jnp.arange(REGIONS, dtype=jnp.int32))


def shard_levels(key, dims, pieces, low, largest):
    loudness = 1.0
    for dim, parts in pieces:
        steps = jax.random.uniform(jax.random.fold_in(jax.random.fold_in(key, 6), dim), (parts,), jnp.float32, low / len(pieces), largest / len(pieces))
        loudness = loudness * jnp.repeat(jnp.exp(steps), dims[dim] // parts).reshape((-1,) + (1,) * (len(dims) - 1 - dim))
    return loudness


def centred(stream_key, extent, deviation, bound, shards=(), kind=jnp.bfloat16):
    gain = shard_levels(stream_key, extent, shards, -0.22, 0.18) if shards else 1.0
    array = jax.random.normal(stream_key, extent, jnp.float32) * deviation * gain
    return jnp.minimum(jnp.maximum(array, -bound), bound).astype(kind)


def setup_inputs(seed: int = 0) -> dict:
    key_list = jax.random.split(jax.random.key(seed), 6)
    return {
        "ensemble": centred(key_list[0], (MEMBERS, FIELDS, LEVELS, NX, CY), 1.0, 6.0, ((0, 16), (3, 32)), jnp.float32),
        "winds": jnp.clip(jax.random.uniform(key_list[1], (2, LEVELS, NX, CY), jnp.float32, -0.35, 0.35) * shard_levels(key_list[1], (2, LEVELS, NX, CY), ((2, 32),), -0.4, 0.0), -0.35, 0.35),
        "diffusion": jnp.clip(jnp.exp(jax.random.uniform(key_list[2], (LEVELS,), jnp.float32, math.log(0.01), math.log(0.07))), 0.01, 0.07),
        "labels": draw_labels(jax.random.fold_in(key_list[5], 71), 0),
        "amplitude": jnp.clip(jnp.exp(jax.random.uniform(key_list[4], (REGIONS,), jnp.float32, math.log(0.5), math.log(2.0))), 0.5, 2.0),
    }


def advance(values, winds, diffusion):
    western = jnp.roll(values, 1, axis=-2)
    eastern = jnp.roll(values, -1, axis=-2)
    widths = [(0, 0)] * (values.ndim - 1) + [(1, 1)]
    padded = jnp.pad(values, widths)
    southern = padded[..., :-2]
    northern = padded[..., 2:]
    wind_east = winds[0]
    wind_north = winds[1]
    advected = jnp.maximum(wind_east, 0.0) * (values - western) + jnp.minimum(wind_east, 0.0) * (eastern - values)
    advected = advected + jnp.maximum(wind_north, 0.0) * (values - southern) + jnp.minimum(wind_north, 0.0) * (northern - values)
    laplace = western + eastern + southern + northern - 4.0 * values
    return values - advected + diffusion.reshape(-1, 1, 1) * laplace

def reference(ensemble, winds, diffusion, labels, amplitude):
    control = advance(advance(ensemble[0], winds, diffusion), winds, diffusion)
    in_region = labels[None, :, :] == jnp.arange(REGIONS, dtype=jnp.int32)[:, None, None]
    counts = lax.optimization_barrier(jnp.sum(in_region.astype(jnp.float32), axis=(1, 2)))

    def one_member(fields):
        advanced = advance(advance(fields, winds, diffusion), winds, diffusion)
        departure = advanced - control
        squares = lax.optimization_barrier(jnp.sum(departure * departure, axis=(0, 1)))
        sums = lax.optimization_barrier(jnp.sum(jnp.where(in_region, squares[None], jnp.float32(0.0)), axis=(1, 2)))
        mean_square = sums / (counts * FIELDS * LEVELS)
        factor = amplitude / jnp.sqrt(mean_square + 1e-06)
        column_scale = lax.optimization_barrier(jnp.sum(jnp.where(in_region, factor[:, None, None], jnp.float32(0.0)), axis=0))
        return control + departure * column_scale
    return lax.map(one_member, ensemble)
```

```python
import functools

import jax
import jax.numpy as jnp
from jax import lax
from jax.experimental import pallas as pl
from jax.experimental.pallas import tpu as pltpu
from jax.sharding import PartitionSpec as P

MESH = pl.DeviceIdType.MESH
DMA = pltpu.SemaphoreType.DMA
TILES = 32
PAD = 8


def kernel(
    ens, winds, diffusion, labels, amplitude, ctl, dep, scale,
    ext, wext, coef, mid, acc, ar,
    load_sem, halo_send, halo_recv, s1_send, s1_recv, cross_send, cross_recv,
    s2_send, s2_recv, sib_send, sib_recv, ar_send, ar_recv,
):
    fields, levels, rows, cols = ctl.shape
    regions = amplitude.shape[0]
    m = lax.axis_index("member")
    t = lax.axis_index("tile")
    x, yh, c = m // 4, (m // 2) % 2, m % 2
    mine = 2 * x + c
    sib = m + 1 - 2 * c
    other_half = m + 2 - 4 * yh

    def mate(k):
        return (m + 4 * k) % 16

    def tile(d):
        return (t + d) % TILES

    def remote(src, dst, send, recv, member, at):
        return pltpu.make_async_remote_copy(
            src_ref=src, dst_ref=dst, send_sem=send, recv_sem=recv,
            device_id=(member, at), device_id_type=MESH,
        )

    own_rows = pl.ds(PAD, rows)
    load_f = pltpu.make_async_copy(ens.at[0], ext.at[:, :, own_rows], load_sem.at[0])
    load_w = pltpu.make_async_copy(winds, wext.at[:, :, own_rows], load_sem.at[1])
    load_f.start()
    load_w.start()

    barrier = pltpu.get_barrier_semaphore()
    near = [mate(1), mate(2), mate(3), sib, other_half]
    near += [(sib + 4 * k) % 16 for k in (1, 2, 3)]
    for member in near:
        pl.semaphore_signal(barrier, inc=1, device_id=(member, t), device_id_type=MESH)
    for d in range(1, TILES):
        pl.semaphore_signal(barrier, inc=1, device_id=(m, tile(d)), device_id_type=MESH)
    pl.semaphore_wait(barrier, len(near) + TILES - 1)

    halos = [
        remote(ens.at[0, :, :, pl.ds(rows - 2, 2)], ext.at[:, :, pl.ds(PAD - 2, 2)],
               halo_send.at[0], halo_recv.at[0], m, tile(1)),
        remote(ens.at[0, :, :, pl.ds(0, 2)], ext.at[:, :, pl.ds(PAD + rows, 2)],
               halo_send.at[1], halo_recv.at[1], m, tile(TILES - 1)),
        remote(winds.at[:, :, pl.ds(rows - 1, 1)], wext.at[:, :, pl.ds(PAD - 1, 1)],
               halo_send.at[2], halo_recv.at[2], m, tile(1)),
        remote(winds.at[:, :, pl.ds(0, 1)], wext.at[:, :, pl.ds(PAD + rows, 1)],
               halo_send.at[3], halo_recv.at[3], m, tile(TILES - 1)),
    ]
    for copy in halos:
        copy.start()
    load_f.wait()
    load_w.wait()
    for copy in halos:
        copy.wait_recv()

    column = lax.broadcasted_iota(jnp.int32, (rows + 2 * PAD, cols), 1)

    def stencil(v, c0, cw, ce, cs, cn):
        n = v.shape[0]
        return (
            c0 * v
            + cw * pltpu.roll(v, 1, 0)
            + ce * pltpu.roll(v, n - 1, 0)
            + cs * pltpu.roll(v, 1, 1)
            + cn * pltpu.roll(v, cols - 1, 1)
        )

    def s1(level):
        holder = (level // 2) * 4 + level % 2
        return remote(dep.at[:, level], ctl.at[:, level], s1_send.at[level], s1_recv, holder, t)

    def advance(level, carry):
        east, north = wext[0, level], wext[1, level]
        k = diffusion[level]
        east_p, east_m = jnp.maximum(east, 0.0), jnp.minimum(east, 0.0)
        north_p, north_m = jnp.maximum(north, 0.0), jnp.minimum(north, 0.0)
        coef[0] = 1.0 - east_p + east_m - north_p + north_m - 4.0 * k
        coef[1] = east_p + k
        coef[2] = k - east_m
        coef[3] = jnp.where(column == 0, 0.0, north_p + k)
        coef[4] = jnp.where(column == cols - 1, 0.0, k - north_m)
        for f in range(fields):
            mid[...] = stencil(ext[f, level], *(coef[i] for i in range(5)))
            new = stencil(mid[...], *(coef[i] for i in range(5)))
            dep[f, level] = new[PAD:PAD + rows]

        @pl.when((m == 0) & (level > 0))
        def _():
            s1(level).start()

        return carry

    lax.fori_loop(0, levels, advance, 0)

    @pl.when(m == 0)
    def _():
        ctl[:, 0] = dep[:, 0]

    @pl.when((m != 0) & (yh == 0))
    def _():
        s1(mine).wait_recv()

    cross = remote(ctl.at[:, mine], ctl.at[:, mine], cross_send, cross_recv, other_half, t)

    @pl.when(yh == 0)
    def _():
        cross.start()

    @pl.when(yh == 1)
    def _():
        cross.wait_recv()

    def from_x(k, core):
        return 2 * ((x + 4 - k) % 4) + core

    def s2(k):
        return remote(ctl.at[:, mine], ctl.at[:, mine], s2_send.at[k], s2_recv.at[k], mate(k), t)

    def s2_arrival(k):
        level = from_x(k, c)
        return remote(ctl.at[:, level], ctl.at[:, level], s2_send.at[k], s2_recv.at[k], mate(k), t)

    def to_sib(k):
        level = from_x(k, c)
        return remote(ctl.at[:, level], ctl.at[:, level], sib_send.at[k], sib_recv.at[k], sib, t)

    def from_sib(k):
        level = from_x(k, 1 - c)
        return remote(ctl.at[:, level], ctl.at[:, level], sib_send.at[k], sib_recv.at[k], sib, t)

    @pl.when(m == 0)
    def _():
        for level in range(1, levels):
            s1(level).wait_send()

    for k in (2, 1, 3):
        s2(k).start()
    to_sib(0).start()
    acc[...] = jnp.zeros_like(acc)

    def add_squares(level):
        total = acc[...]
        for f in range(fields):
            d = dep[f, level] - ctl[f, level]
            dep[f, level] = d
            total = total + d * d
        acc[...] = total

    add_squares(mine)
    for k in (1, 3, 2):
        s2_arrival(k).wait_recv()
        to_sib(k).start()
        add_squares(from_x(k, c))
    for k in (0, 1, 3, 2):
        from_sib(k).wait_recv()
        add_squares(from_x(k, 1 - c))

    lane = lax.broadcasted_iota(jnp.int32, (8, 128), 1)
    sub = lax.broadcasted_iota(jnp.int32, (8, 128), 0)
    block = jnp.zeros((8, 128), jnp.float32)
    squares = acc[...]
    where_label = labels[...]
    target = jnp.zeros((8, 128), jnp.float32)
    for r in range(regions):
        hit = where_label == r
        total = jnp.sum(jnp.where(hit, squares, 0.0))
        count = jnp.sum(hit.astype(jnp.float32))
        row, at = sub == r % 8, r // 8
        block = jnp.where(row & (lane == at), total, block)
        block = jnp.where(row & (lane == at + 2), count, block)
        target = jnp.where(row & (lane == at), amplitude[r], target)
    ar[0] = block

    def ar_copy(d):
        return remote(ar.at[0], ar.at[d], ar_send, ar_recv, m, tile(d))

    for d in range(1, TILES):
        ar_copy(d).start()
    rest = ar.at[pl.ds(1, TILES - 1)]
    pltpu.make_async_copy(rest, rest, ar_recv).wait()
    total = jnp.sum(ar[...], axis=0)
    counts = pltpu.roll(total, 126, 1)
    counts = jnp.where(lane < 2, counts, 1.0)
    factor = target / jnp.sqrt(total / (counts * (fields * levels)) + 1e-06)
    scales = jnp.zeros((rows, cols), jnp.float32)
    for r in range(regions):
        value = factor[r % 8:r % 8 + 1, r // 8:r // 8 + 1]
        scales = jnp.where(where_label == r, value, scales)
    scale[...] = scales

    pltpu.make_async_copy(rest, rest, ar_send).wait()
    for copy in halos:
        copy.wait_send()

    @pl.when(yh == 0)
    def _():
        cross.wait_send()

    for k in (1, 2, 3):
        s2(k).wait_send()
    for k in range(4):
        to_sib(k).wait_send()


def on_device(ensemble, winds, diffusion, labels, amplitude):
    _, fields, levels, rows, cols = ensemble.shape
    block = jax.ShapeDtypeStruct((fields, levels, rows, cols), jnp.float32)
    f32 = jnp.float32
    tall = rows + 2 * PAD
    vmem = pl.BlockSpec(memory_space=pltpu.VMEM)
    smem = pl.BlockSpec(memory_space=pltpu.SMEM)
    hbm = pl.BlockSpec(memory_space=pl.ANY)
    control, departure, scale = pl.pallas_call(
        kernel,
        name="breed",
        out_shape=(block, block, jax.ShapeDtypeStruct((rows, cols), f32)),
        in_specs=[hbm, hbm, smem, vmem, smem],
        out_specs=(vmem, vmem, vmem),
        scratch_shapes=[
            pltpu.VMEM((fields, levels, tall, cols), f32),
            pltpu.VMEM((2, levels, tall, cols), f32),
            pltpu.VMEM((5, tall, cols), f32),
            pltpu.VMEM((tall, cols), f32),
            pltpu.VMEM((rows, cols), f32),
            pltpu.VMEM((TILES, 8, 128), f32),
            DMA((2,)), DMA((4,)), DMA((4,)), DMA((levels,)), DMA, DMA, DMA,
            DMA((4,)), DMA((4,)), DMA((4,)), DMA((4,)), DMA, DMA,
        ],
        compiler_params=pltpu.CompilerParams(
            collective_id=0, has_side_effects=True, vmem_limit_bytes=32 * 2**20
        ),
    )(ensemble, winds, diffusion, labels, amplitude)
    return (control + departure * scale)[None]


def solution(mesh):
    return jax.shard_map(
        on_device,
        mesh=mesh,
        in_specs=(
            P("member", None, None, "tile", None),
            P(None, None, "tile", None),
            P(),
            P("tile", None),
            P(),
        ),
        out_specs=P("member", None, None, "tile", None),
        check_vma=False,
    )
```

```python
import jax
import jax.numpy as jnp
from jax import lax
from jax.experimental import pallas as pl
from jax.experimental.pallas import tpu as pltpu
from jax.sharding import PartitionSpec as P

MESH = pl.DeviceIdType.MESH
DMA = pltpu.SemaphoreType.DMA
TILES = 32


def kernel(
    ens, winds, diffusion_in, labels_in, amplitude_in, ctl, dep, scale,
    ext, wext, cext, coef, mid, acc, ar, diffusion, labels, amplitude,
    load_sem, halo_send, halo_recv, s1_send, s1_recv, cross_send, cross_recv,
    s2_send, s2_recv, sib_send, sib_recv, edge_send, edge_recv,
    e2_send, e2_recv, esib_send, esib_recv, ar_send, ar_recv,
):
    fields, levels, rows, cols = ctl.shape
    tall = ext.shape[2]
    regions = amplitude.shape[0]
    m = lax.axis_index("member")
    t = lax.axis_index("tile")
    x, yh, c = m // 4, (m // 2) % 2, m % 2
    mine = 2 * x + c
    sib = m + 1 - 2 * c
    other_half = m + 2 - 4 * yh
    every = range(fields)

    def mate(k):
        return (m + 4 * k) % 16

    def tile(d):
        return (t + d) % TILES

    def remote(src, dst, send, recv, member, at):
        return pltpu.make_async_remote_copy(
            src_ref=src, dst_ref=dst, send_sem=send, recv_sem=recv,
            device_id=(member, at), device_id_type=MESH,
        )

    own = pl.ds(0, rows)
    loads = [
        pltpu.make_async_copy(ens.at[0], ext.at[:, :, own], load_sem.at[0]),
        pltpu.make_async_copy(winds, wext.at[:, :, own], load_sem.at[1]),
        pltpu.make_async_copy(diffusion_in, diffusion, load_sem.at[2]),
        pltpu.make_async_copy(labels_in, labels, load_sem.at[3]),
        pltpu.make_async_copy(amplitude_in, amplitude, load_sem.at[4]),
    ]
    for copy in loads:
        copy.start()
    root_load = pltpu.make_async_copy(ens.at[0, :, 0], cext.at[:, 0, own], load_sem.at[5])

    @pl.when(m == 0)
    def _():
        root_load.start()

    barrier = pltpu.get_barrier_semaphore()
    near = [mate(1), mate(2), mate(3), sib, other_half]
    near += [(sib + 4 * k) % 16 for k in (1, 2, 3)]
    for d in range(1, TILES):
        pl.semaphore_signal(barrier, inc=1, device_id=(m, tile(d)), device_id_type=MESH)
    for member in near:
        pl.semaphore_signal(barrier, inc=1, device_id=(member, t), device_id_type=MESH)
    pl.semaphore_wait(barrier, len(near) + TILES - 1)

    def s1(level, f):
        holder = (level // 2) * 4 + level % 2
        return remote(ens.at[0, f, level], cext.at[f, level, own],
                      s1_send.at[level, f], s1_recv.at[f], holder, t)

    @pl.when(m == 0)
    def _():
        for f in every:
            for level in (4, 5, 2, 3, 6, 7, 1):
                s1(level, f).start()

    last, first = pl.ds(rows - 2, 2), pl.ds(0, 2)
    low, high = pl.ds(tall - 2, 2), pl.ds(rows, 2)
    halos = [
        remote(winds.at[:, :, pl.ds(rows - 1, 1)], wext.at[:, :, pl.ds(tall - 1, 1)],
               halo_send.at[2], halo_recv.at[2], m, tile(1)),
        remote(winds.at[:, :, pl.ds(0, 1)], wext.at[:, :, pl.ds(rows, 1)],
               halo_send.at[3], halo_recv.at[3], m, tile(TILES - 1)),
        remote(ens.at[0, :, :, last], ext.at[:, :, low],
               halo_send.at[0], halo_recv.at[0], m, tile(1)),
        remote(ens.at[0, :, :, first], ext.at[:, :, high],
               halo_send.at[1], halo_recv.at[1], m, tile(TILES - 1)),
    ]
    for copy in halos:
        copy.start()

    def cross(f):
        at = cext.at[f, mine, own]
        return remote(at, at, cross_send.at[f], cross_recv.at[f], other_half, t)

    def level_of(k, core):
        return 2 * ((x + 4 - k) % 4) + core

    def s2(k, f):
        at = cext.at[f, mine, own]
        return remote(at, at, s2_send.at[k, f], s2_recv.at[k, f], mate(k), t)

    def s2_in(k, f):
        at = cext.at[f, level_of(k, c), own]
        return remote(at, at, s2_send.at[k, f], s2_recv.at[k, f], mate(k), t)

    def to_sib(k, f):
        at = cext.at[f, level_of(k, c), own]
        return remote(at, at, sib_send.at[k, f], sib_recv.at[k, f], sib, t)

    def from_sib(k, f):
        at = cext.at[f, level_of(k, 1 - c), own]
        return remote(at, at, sib_send.at[k, f], sib_recv.at[k, f], sib, t)

    @pl.when(m == 0)
    def _():
        root_load.wait()

    for f in every:
        @pl.when((m != 0) & (yh == 0))
        def _():
            s1(mine, f).wait_recv()

        @pl.when(yh == 0)
        def _():
            cross(f).start()

        @pl.when(yh == 1)
        def _():
            cross(f).wait_recv()

        for k in (2, 1, 3):
            s2(k, f).start()
        to_sib(0, f).start()

    edges = [
        remote(cext.at[:, mine, last], cext.at[:, mine, low],
               edge_send.at[0], edge_recv.at[0], m, tile(1)),
        remote(cext.at[:, mine, first], cext.at[:, mine, high],
               edge_send.at[1], edge_recv.at[1], m, tile(TILES - 1)),
    ]
    for copy in edges:
        copy.start()

    for copy in loads:
        copy.wait()
    for copy in halos[:2]:
        copy.wait_recv()

    column = lax.broadcasted_iota(jnp.int32, (tall, cols), 1)

    def weigh(level, carry):
        east, north = wext[0, level], wext[1, level]
        k = diffusion[level]
        east_p, east_m = jnp.maximum(east, 0.0), jnp.minimum(east, 0.0)
        north_p, north_m = jnp.maximum(north, 0.0), jnp.minimum(north, 0.0)
        coef[level, 0] = 1.0 - east_p + east_m - north_p + north_m - 4.0 * k
        coef[level, 1] = east_p + k
        coef[level, 2] = k - east_m
        coef[level, 3] = jnp.where(column == 0, 0.0, north_p + k)
        coef[level, 4] = jnp.where(column == cols - 1, 0.0, k - north_m)
        return carry

    lax.fori_loop(0, levels, weigh, 0)

    def step(v, level):
        return (
            coef[level, 0] * v
            + coef[level, 1] * pltpu.roll(v, 1, 0)
            + coef[level, 2] * pltpu.roll(v, tall - 1, 0)
            + coef[level, 3] * pltpu.roll(v, 1, 1)
            + coef[level, 4] * pltpu.roll(v, cols - 1, 1)
        )

    def two_steps(v, level):
        mid[...] = step(v, level)
        return step(mid[...], level)[:rows]

    for copy in halos[2:]:
        copy.wait_recv()

    def advance(level, carry):
        for f in every:
            dep[f, level] = two_steps(ext[f, level], level)
        return carry

    lax.fori_loop(0, levels, advance, 0)

    for f in every:
        for k in (1, 3, 2):
            s2_in(k, f).wait_recv()
            to_sib(k, f).start()

    def e2(k, side):
        at = cext.at[:, mine, (low, high)[side]]
        return remote(at, at, e2_send.at[k, side], e2_recv.at[k, side], mate(k), t)

    def e2_in(k, side):
        at = cext.at[:, level_of(k, c), (low, high)[side]]
        return remote(at, at, e2_send.at[k, side], e2_recv.at[k, side], mate(k), t)

    def edge_to_sib(k, side):
        at = cext.at[:, level_of(k, c), (low, high)[side]]
        return remote(at, at, esib_send.at[k, side], esib_recv.at[k, side], sib, t)

    def edge_from_sib(k, side):
        at = cext.at[:, level_of(k, 1 - c), (low, high)[side]]
        return remote(at, at, esib_send.at[k, side], esib_recv.at[k, side], sib, t)

    for side in (0, 1):
        edges[side].wait_recv()
        for k in (2, 1, 3):
            e2(k, side).start()
        edge_to_sib(0, side).start()

    acc[...] = jnp.zeros_like(acc)

    def depart(level):
        def one(f, carry):
            control = two_steps(cext[f, level], level)
            d = dep[f, level] - control
            ctl[f, level] = control
            dep[f, level] = d
            acc[...] = acc[...] + d * d
            return carry

        lax.fori_loop(0, fields, one, 0)

    depart(mine)
    for k in (1, 3, 2):
        for side in (0, 1):
            e2_in(k, side).wait_recv()
            edge_to_sib(k, side).start()
        depart(level_of(k, c))
    for k in (0, 1, 3, 2):
        for f in every:
            from_sib(k, f).wait_recv()
        for side in (0, 1):
            edge_from_sib(k, side).wait_recv()
        depart(level_of(k, 1 - c))

    lane = lax.broadcasted_iota(jnp.int32, (8, 128), 1)
    sub = lax.broadcasted_iota(jnp.int32, (8, 128), 0)
    block = jnp.zeros((8, 128), jnp.float32)
    squares = acc[...]
    where_label = labels[...]
    target = jnp.zeros((8, 128), jnp.float32)
    for r in range(regions):
        hit = where_label == r
        total = jnp.sum(jnp.where(hit, squares, 0.0))
        count = jnp.sum(hit.astype(jnp.float32))
        row, at = sub == r % 8, r // 8
        block = jnp.where(row & (lane == at), total, block)
        block = jnp.where(row & (lane == at + 2), count, block)
        target = jnp.where(row & (lane == at), amplitude[r], target)
    ar[0] = block

    def ar_copy(d):
        return remote(ar.at[0], ar.at[d], ar_send, ar_recv, m, tile(d))

    for d in range(1, TILES):
        ar_copy(d).start()
    rest = ar.at[pl.ds(1, TILES - 1)]
    pltpu.make_async_copy(rest, rest, ar_recv).wait()
    total = jnp.sum(ar[...], axis=0)
    counts = pltpu.roll(total, 126, 1)
    counts = jnp.where(lane < 2, counts, 1.0)
    factor = target / jnp.sqrt(total / (counts * (fields * levels)) + 1e-06)
    scales = jnp.zeros((rows, cols), jnp.float32)
    for r in range(regions):
        value = factor[r % 8:r % 8 + 1, r // 8:r // 8 + 1]
        scales = jnp.where(where_label == r, value, scales)
    scale[...] = scales

    pltpu.make_async_copy(rest, rest, ar_send).wait()
    for copy in halos + edges:
        copy.wait_send()
    for f in every:
        @pl.when(m == 0)
        def _():
            for level in range(1, levels):
                s1(level, f).wait_send()

        @pl.when(yh == 0)
        def _():
            cross(f).wait_send()

        for k in (1, 2, 3):
            s2(k, f).wait_send()
        for k in range(4):
            to_sib(k, f).wait_send()
    for side in (0, 1):
        for k in (1, 2, 3):
            e2(k, side).wait_send()
        for k in range(4):
            edge_to_sib(k, side).wait_send()


def on_device(ensemble, winds, diffusion, labels, amplitude):
    _, fields, levels, rows, cols = ensemble.shape
    block = jax.ShapeDtypeStruct((fields, levels, rows, cols), jnp.float32)
    f32 = jnp.float32
    tall = rows + 8
    vmem = pl.BlockSpec(memory_space=pltpu.VMEM)
    hbm = pl.BlockSpec(memory_space=pltpu.HBM)
    inputs = [
        pltpu.with_memory_space_constraint(a, pltpu.HBM)
        for a in (ensemble, winds, diffusion, labels, amplitude)
    ]
    pair = (DMA((4, 2)), DMA((4, 2)))
    control, departure, scale = pl.pallas_call(
        kernel,
        name="breed",
        out_shape=(block, block, jax.ShapeDtypeStruct((rows, cols), f32)),
        in_specs=[hbm] * 5,
        out_specs=(vmem, vmem, vmem),
        scratch_shapes=[
            pltpu.VMEM((fields, levels, tall, cols), f32),
            pltpu.VMEM((2, levels, tall, cols), f32),
            pltpu.VMEM((fields, levels, tall, cols), f32),
            pltpu.VMEM((levels, 5, tall, cols), f32),
            pltpu.VMEM((tall, cols), f32),
            pltpu.VMEM((rows, cols), f32),
            pltpu.VMEM((TILES, 8, 128), f32),
            pltpu.SMEM((levels,), f32),
            pltpu.VMEM((rows, cols), jnp.int32),
            pltpu.SMEM(amplitude.shape, f32),
            DMA((6,)), DMA((4,)), DMA((4,)), DMA((levels, fields)), DMA((fields,)),
            DMA((fields,)), DMA((fields,)),
            DMA((4, fields)), DMA((4, fields)), DMA((4, fields)), DMA((4, fields)),
            DMA((2,)), DMA((2,)), *pair, *pair, DMA, DMA,
        ],
        compiler_params=pltpu.CompilerParams(
            collective_id=0, has_side_effects=True, vmem_limit_bytes=32 * 2**20
        ),
    )(*inputs)
    return (control + departure * scale)[None]


def solution(mesh):
    return jax.shard_map(
        on_device,
        mesh=mesh,
        in_specs=(
            P("member", None, None, "tile", None),
            P(None, None, "tile", None),
            P(),
            P("tile", None),
            P(),
        ),
        out_specs=P("member", None, None, "tile", None),
        check_vma=False,
    )
```

```python
import jax
import jax.numpy as jnp
from jax import lax
from jax.experimental import pallas as pl
from jax.experimental.pallas import tpu as pltpu
from jax.sharding import PartitionSpec as P

MESH = pl.DeviceIdType.MESH
DMA = pltpu.SemaphoreType.DMA
TILES = 32


def kernel(
    ens, winds, diffusion_in, labels_in, amplitude_in, ctl, dep, scale,
    ext, wext, cext, cown, fix, coef, mid, acc, rim, part, ar, diffusion, labels, amplitude,
    load_sem, halo_send, halo_recv, wind_send, wind_recv,
    root_send, pair_send, pair_recv, hop_send, cross_send, s2_send, sib_send, main_recv,
    edge_send, edge_recv, e2_send, e2_recv, esib_send, esib_recv, ar_send, ar_recv,
):
    fields, levels, rows, cols = ctl.shape
    tall = ext.shape[2]
    regions = amplitude.shape[0]
    m = lax.axis_index("member")
    t = lax.axis_index("tile")
    x, yh, c = m // 4, (m // 2) % 2, m % 2
    mine = 2 * x + c
    sib = m + 1 - 2 * c
    other_half = m + 2 - 4 * yh
    every = range(fields)

    def mate(k):
        return (m + 4 * k) % 16

    def tile(d):
        return (t + d) % TILES

    def remote(src, dst, send, recv, member, at):
        return pltpu.make_async_remote_copy(
            src_ref=src, dst_ref=dst, send_sem=send, recv_sem=recv,
            device_id=(member, at), device_id_type=MESH,
        )

    own = pl.ds(0, rows)
    loads = [
        pltpu.make_async_copy(ens.at[0], ext.at[:, :, own], load_sem.at[0]),
        pltpu.make_async_copy(winds, wext.at[:, :, own], load_sem.at[1]),
        pltpu.make_async_copy(diffusion_in, diffusion, load_sem.at[2]),
        pltpu.make_async_copy(labels_in, labels, load_sem.at[3]),
        pltpu.make_async_copy(amplitude_in, amplitude, load_sem.at[4]),
    ]
    for copy in loads:
        copy.start()
    root_load = pltpu.make_async_copy(ens.at[0], cext, load_sem.at[5])

    @pl.when(m == 0)
    def _():
        root_load.start()

    barrier = pltpu.get_barrier_semaphore()
    near = [mate(1), mate(2), mate(3), sib, other_half, sib + 2 - 4 * yh]
    near += [(sib + 4 * k) % 16 for k in (1, 2, 3)]
    for member in near:
        pl.semaphore_signal(barrier, inc=1, device_id=(member, t), device_id_type=MESH)
    for d in range(1, TILES):
        pl.semaphore_signal(barrier, inc=1, device_id=(m, tile(d)), device_id_type=MESH)
    pl.semaphore_wait(barrier, len(near) + TILES - 1)

    def up(core):
        return [(2, 0), (2 * (1 - core), 1), (1, 0), (1, 1), (1, 2), (0, 0)]

    def down(core):
        return [(2, 2), (2 * core, 1), (3, 0), (3, 1), (3, 2), (0, 2)]

    def plane(f, level):
        return cext.at[f, level]

    def arrival(f, level):
        at = plane(f, level)
        return remote(at, at, hop_send.at[f, level], main_recv.at[f, level], sib, t)

    def pass_on(f, level, member):
        at = plane(f, level)
        return remote(at, at, hop_send.at[f, level], main_recv.at[f, level], member, t)

    def cross(f):
        at = plane(f, mine)
        return remote(at, at, cross_send.at[0, f], main_recv.at[f, mine], other_half, t)

    def to_sib(f, level):
        at = plane(f, level)
        return remote(at, at, sib_send.at[f, level], main_recv.at[f, level], sib, t)

    def root_chain(f, level, member):
        return remote(ens.at[0, f, level], plane(f, level),
                      root_send.at[f, level], main_recv.at[f, level], member, t)

    def root_cross(f, level):
        return remote(ens.at[0, f, level], plane(f, level),
                      cross_send.at[level, f], main_recv.at[f, level], 2 + level, t)

    def root_pair(f):
        return remote(ens.at[0, f], cext.at[f], pair_send.at[f], pair_recv.at[f], 1, t)

    @pl.when(m == 0)
    def _():
        for i in range(6):
            for core in (0, 1):
                q, f = up(core)[i]
                root_chain(f, 2 * q + core, 4 + core).start()
                q, f = down(core)[i]
                root_chain(f, 2 * q + core, 12 + core).start()
            if i < fields:
                for core in (0, 1):
                    root_cross(i, core).start()
        for f in every:
            root_pair(f).start()

    last, first = pl.ds(rows - 2, 2), pl.ds(0, 2)
    low, high = pl.ds(tall - 2, 2), pl.ds(rows, 2)
    wind_last, wind_first = pl.ds(rows - 1, 1), pl.ds(0, 1)
    wind_low, wind_high = pl.ds(tall - 1, 1), pl.ds(rows, 1)
    halos = [
        remote(winds.at[c, :, wind_last], wext.at[c, :, wind_low],
               halo_send.at[2], halo_recv.at[2], m, tile(1)),
        remote(winds.at[c, :, wind_first], wext.at[c, :, wind_high],
               halo_send.at[3], halo_recv.at[3], m, tile(TILES - 1)),
        remote(ens.at[0, :, :, last], ext.at[:, :, low],
               halo_send.at[0], halo_recv.at[0], m, tile(1)),
        remote(ens.at[0, :, :, first], ext.at[:, :, high],
               halo_send.at[1], halo_recv.at[1], m, tile(TILES - 1)),
    ]
    for copy in halos:
        copy.start()

    def level_of(k, core):
        return 2 * ((x + 4 - k) % 4) + core

    def s2(k, f):
        at = plane(f, mine)
        return remote(at, at, s2_send.at[k, f], main_recv.at[f, mine], mate(k), t)

    edges = [
        remote(cext.at[:, mine, last], cown.at[:, low],
               edge_send.at[0], edge_recv.at[0], m, tile(1)),
        remote(cext.at[:, mine, first], cown.at[:, high],
               edge_send.at[1], edge_recv.at[1], m, tile(TILES - 1)),
    ]
    def start_edges():
        for copy in edges:
            copy.start()

    def along(plane_of, member):
        q, f = plane_of
        level = 2 * q + c
        arrival(f, level).wait_recv()
        if member is not None:
            pass_on(f, level, member).start()
        to_sib(f, level).start()

    @pl.when(m == 0)
    def _():
        root_load.wait()
        start_edges()

    @pl.when(m == 1)
    def _():
        for f in every:
            root_pair(f).wait_recv()
        start_edges()

    @pl.when((yh == 0) & (x == 1))
    def _():
        for i, p in enumerate(up(c)):
            along(p, 8 + c)
            if 2 <= i < 5:
                cross(i - 2).start()
            if i == 4:
                start_edges()
        for p in down(c):
            along(p, None)

    @pl.when((yh == 0) & (x == 3))
    def _():
        for i, p in enumerate(down(c)):
            along(p, 8 + c)
            if 2 <= i < 5:
                cross(i - 2).start()
            if i == 4:
                start_edges()
        for p in up(c):
            along(p, None)

    @pl.when((yh == 0) & (x == 2))
    def _():
        for i, (p, n) in enumerate(zip(up(c), down(c))):
            along(p, 12 + c)
            if i == 0:
                cross(0).start()
            along(n, 4 + c)
            if i == 0:
                cross(2).start()
            if i == 1:
                cross(1).start()
                start_edges()

    @pl.when(yh == 1)
    def _():
        for f in every:
            arrival(f, mine).wait_recv()
            for k in (2, 1, 3):
                s2(k, f).start()
            to_sib(f, mine).start()
        start_edges()

    for copy in loads:
        copy.wait()
    wind_pair = [
        remote(wext.at[c, :, at], wext.at[c, :, at], wind_send.at[i], wind_recv.at[i], sib, t)
        for i, at in enumerate((wind_low, wind_high))
    ]
    for copy, pair in zip(halos[:2], wind_pair):
        copy.wait_recv()
        pair.start()
    for i, at in enumerate((wind_low, wind_high)):
        there = wext.at[1 - c, :, at]
        remote(there, there, wind_send.at[i], wind_recv.at[i], sib, t).wait_recv()

    column = lax.broadcasted_iota(jnp.int32, (tall, cols), 1)

    def weigh(level, carry):
        east, north = wext[0, level], wext[1, level]
        k = diffusion[level]
        east_p, east_m = jnp.maximum(east, 0.0), jnp.minimum(east, 0.0)
        north_p, north_m = jnp.maximum(north, 0.0), jnp.minimum(north, 0.0)
        coef[level, 0] = 1.0 - east_p + east_m - north_p + north_m - 4.0 * k
        coef[level, 1] = east_p + k
        coef[level, 2] = k - east_m
        coef[level, 3] = jnp.where(column == 0, 0.0, north_p + k)
        coef[level, 4] = jnp.where(column == cols - 1, 0.0, k - north_m)
        return carry

    lax.fori_loop(0, levels, weigh, 0)

    def step(v, level):
        n = v.shape[0]
        return (
            coef[level, 0, :n] * v
            + coef[level, 1, :n] * pltpu.roll(v, 1, 0)
            + coef[level, 2, :n] * pltpu.roll(v, n - 1, 0)
            + coef[level, 3, :n] * pltpu.roll(v, 1, 1)
            + coef[level, 4, :n] * pltpu.roll(v, cols - 1, 1)
        )

    def two_steps(v, level):
        n = v.shape[0]
        mid[:n] = step(v, level)
        return step(mid[:n], level)[:rows]

    for copy in halos[2:]:
        copy.wait_recv()

    sub = lax.broadcasted_iota(jnp.int32, (8, cols), 0)
    acc[...] = jnp.zeros_like(acc)

    def advance(level, carry):
        for f in every:
            new = two_steps(ext[f, level], level)
            dep[f, level] = new
            rim[f, level] = jnp.where(sub < 4, new[:8], new[8:])
        return carry

    lax.fori_loop(0, levels, advance, 0)

    def gather(f):
        @pl.when(yh == 1)
        def _():
            for k in (1, 3, 2):
                arrival(f, level_of(k, c)).wait_recv()
                to_sib(f, level_of(k, c)).start()

    gather(0)
    gather(1)

    def rows_of(ref, level, side):
        if ref is fix:
            return fix.at[:, level, (pl.ds(0, 2), pl.ds(6, 2))[side]]
        return ctl.at[:, level, (first, last)[side]]

    def e2(k, side):
        return remote(rows_of(ctl, mine, side), rows_of(fix, mine, side),
                      e2_send.at[k, side], e2_recv.at[k, side], mate(k), t)

    def e2_in(k, side):
        at = rows_of(fix, level_of(k, c), side)
        return remote(at, at, e2_send.at[k, side], e2_recv.at[k, side], mate(k), t)

    def edge_to_sib(k, side):
        level = level_of(k, c)
        return remote(rows_of(fix if k else ctl, level, side), rows_of(fix, level, side),
                      esib_send.at[k, side], esib_recv.at[k, side], sib, t)

    def edge_from_sib(k, side):
        at = rows_of(fix, level_of(k, 1 - c), side)
        return remote(at, at, esib_send.at[k, side], esib_recv.at[k, side], sib, t)

    for side in (0, 1):
        edges[side].wait_recv()

    def own_level(f, carry):
        cown[f, :rows] = cext[f, mine]
        control = two_steps(cown[f], mine)
        ctl[f, mine] = control
        fix[f, mine] = jnp.where(sub < 4, control[:8], control[8:])
        d = dep[f, mine] - control
        dep[f, mine] = d
        acc[...] = acc[...] + d * d
        return carry

    lax.fori_loop(0, fields, own_level, 0)
    for side in (0, 1):
        for k in (2, 1, 3):
            e2(k, side).start()
        edge_to_sib(0, side).start()

    def other_levels(f):
        @pl.when((yh == 1) | (x > 0))
        def _():
            for k in range(4):
                arrival(f, level_of(k, 1 - c)).wait_recv()

        def one(i, carry):
            level = (mine + 1 + i) % levels
            control = two_steps(cext[f, level], level)
            ctl[f, level] = control
            d = dep[f, level] - control
            dep[f, level] = d
            acc[...] = acc[...] + d * d
            return carry

        lax.fori_loop(0, levels - 1, one, 0)

    other_levels(0)
    other_levels(1)
    gather(2)
    other_levels(2)

    def blocks(v):
        return sum(v[:, 128 * i:128 * (i + 1)] for i in range(cols // 128))

    def along_lanes(offset):
        sums = jnp.sum(jnp.sum(part[...], axis=1), axis=1, keepdims=True)
        lane = lax.broadcasted_iota(jnp.int32, (regions, 128), 1)
        region = lax.broadcasted_iota(jnp.int32, (regions, 128), 0)
        return jnp.sum(jnp.where(lane == region + offset, sums, 0.0), axis=0, keepdims=True)

    lane = lax.broadcasted_iota(jnp.int32, (1, 128), 1)
    target = jnp.zeros((1, 128), jnp.float32)
    outer = (sub < 2) | (sub >= 6)
    where_label = labels[...]
    for r in range(regions):
        one = (where_label == r).astype(jnp.float32)
        part[r] = blocks(one[:8] + one[8:])
        target = jnp.where(lane == r, amplitude[r], target)
    counts = along_lanes(regions)
    top = jnp.where(sub < 2, 0.0, acc[:8])
    bottom = jnp.where(sub >= 6, 0.0, acc[8:])
    for r in range(regions):
        part[r] = blocks(
            jnp.where(where_label[:8] == r, top, 0.0) + jnp.where(where_label[8:] == r, bottom, 0.0)
        )

    def depart(level, total):
        for f in every:
            d = rim[f, level] - fix[f, level]
            total = total + d * d
        return total

    total = depart(mine, jnp.zeros((8, cols), jnp.float32))
    for k in (1, 3, 2):
        for side in (0, 1):
            e2_in(k, side).wait_recv()
            edge_to_sib(k, side).start()
        total = depart(level_of(k, c), total)
    for k in (0, 1, 3, 2):
        for side in (0, 1):
            edge_from_sib(k, side).wait_recv()
        total = depart(level_of(k, 1 - c), total)
    label_rim = jnp.where(sub < 4, where_label[:8], where_label[8:])
    label_rim = jnp.where(outer, label_rim, -1)
    for r in range(regions):
        part[r] = part[r] + blocks(jnp.where(label_rim == r, total, 0.0))
    ar[0] = along_lanes(0) + counts

    def ar_copy(d):
        return remote(ar.at[0], ar.at[d], ar_send, ar_recv, m, tile(d))

    far_first = sorted(range(1, TILES), key=lambda d: abs(d - TILES // 2))
    for d in far_first:
        ar_copy(d).start()

    def patch(i, carry):
        level = (mine + 1 + i) % levels
        for f in every:
            edge = fix[f, level]
            d = rim[f, level] - edge
            ctl[f, level, :8] = jnp.where(sub < 2, edge, ctl[f, level, :8])
            ctl[f, level, 8:] = jnp.where(sub >= 6, edge, ctl[f, level, 8:])
            dep[f, level, :8] = jnp.where(sub < 2, d, dep[f, level, :8])
            dep[f, level, 8:] = jnp.where(sub >= 6, d, dep[f, level, 8:])
        return carry

    lax.fori_loop(0, levels - 1, patch, 0)
    rest = ar.at[pl.ds(1, TILES - 1)]
    pltpu.make_async_copy(rest, rest, ar_recv).wait()
    total = jnp.sum(ar[...], axis=0)
    counts = pltpu.roll(total, 128 - regions, 1)
    counts = jnp.where(lane < regions, counts, 1.0)
    factor = target / jnp.sqrt(total / (counts * (fields * levels)) + 1e-06)
    scales = jnp.zeros((rows, cols), jnp.float32)
    for r in range(regions):
        scales = jnp.where(where_label == r, factor[:, r:r + 1], scales)
    scale[...] = scales

    pltpu.make_async_copy(rest, rest, ar_send).wait()
    for copy in halos + edges + wind_pair:
        copy.wait_send()

    @pl.when(m == 0)
    def _():
        for f in every:
            for level in range(levels):
                root_chain(f, level, 4).wait_send()
            for core in (0, 1):
                root_cross(f, core).wait_send()
            root_pair(f).wait_send()

    @pl.when((yh == 1) | (x > 0))
    def _():
        for f in every:
            for k in range(4):
                to_sib(f, 2 * k + c).wait_send()

    @pl.when((yh == 0) & (x > 0))
    def _():
        for f in every:
            cross(f).wait_send()

    @pl.when((yh == 0) & ((x == 1) | (x == 2)))
    def _():
        for q, f in up(c):
            pass_on(f, 2 * q + c, sib).wait_send()

    @pl.when((yh == 0) & ((x == 3) | (x == 2)))
    def _():
        for q, f in down(c):
            pass_on(f, 2 * q + c, sib).wait_send()

    @pl.when(yh == 1)
    def _():
        for f in every:
            for k in (1, 2, 3):
                s2(k, f).wait_send()

    for side in (0, 1):
        for k in (1, 2, 3):
            e2(k, side).wait_send()
        for k in range(4):
            edge_to_sib(k, side).wait_send()


def on_device(ensemble, winds, diffusion, labels, amplitude):
    _, fields, levels, rows, cols = ensemble.shape
    block = jax.ShapeDtypeStruct((fields, levels, rows, cols), jnp.float32)
    f32 = jnp.float32
    tall = rows + 8
    vmem = pl.BlockSpec(memory_space=pltpu.VMEM)
    hbm = pl.BlockSpec(memory_space=pltpu.HBM)
    inputs = [
        pltpu.with_memory_space_constraint(a, pltpu.HBM)
        for a in (ensemble, winds, diffusion, labels, amplitude)
    ]
    pair = (DMA((4, 2)), DMA((4, 2)))
    planes = DMA((fields, levels))
    control, departure, scale = pl.pallas_call(
        kernel,
        name="breed",
        out_shape=(block, block, jax.ShapeDtypeStruct((rows, cols), f32)),
        in_specs=[hbm] * 5,
        out_specs=(vmem, vmem, vmem),
        scratch_shapes=[
            pltpu.VMEM((fields, levels, tall, cols), f32),
            pltpu.VMEM((2, levels, tall, cols), f32),
            pltpu.VMEM((fields, levels, rows, cols), f32),
            pltpu.VMEM((fields, tall, cols), f32),
            pltpu.VMEM((fields, levels, 8, cols), f32),
            pltpu.VMEM((levels, 5, tall, cols), f32),
            pltpu.VMEM((tall, cols), f32),
            pltpu.VMEM((rows, cols), f32),
            pltpu.VMEM((fields, levels, 8, cols), f32),
            pltpu.VMEM((amplitude.shape[0], 8, 128), f32),
            pltpu.VMEM((TILES, 1, 128), f32),
            pltpu.SMEM((levels,), f32),
            pltpu.VMEM((rows, cols), jnp.int32),
            pltpu.SMEM(amplitude.shape, f32),
            DMA((6,)), DMA((4,)), DMA((4,)), DMA((2,)), DMA((2,)),
            planes, DMA((fields,)), DMA((fields,)), planes, DMA((2, fields)),
            DMA((4, fields)), planes, planes,
            DMA((2,)), DMA((2,)), *pair, *pair, DMA, DMA,
        ],
        compiler_params=pltpu.CompilerParams(
            collective_id=0, has_side_effects=True, vmem_limit_bytes=32 * 2**20
        ),
    )(*inputs)
    return (control + departure * scale)[None]


def solution(mesh):
    return jax.shard_map(
        on_device,
        mesh=mesh,
        in_specs=(
            P("member", None, None, "tile", None),
            P(None, None, "tile", None),
            P(),
            P("tile", None),
            P(),
        ),
        out_specs=P("member", None, None, "tile", None),
        check_vma=False,
    )
```

```python
import jax
import jax.numpy as jnp
from jax import lax
from jax.experimental import pallas as pl
from jax.experimental.pallas import tpu as pltpu
from jax.sharding import PartitionSpec as P

MESH = pl.DeviceIdType.MESH
DMA = pltpu.SemaphoreType.DMA
TILES = 32


def kernel(
    ens, winds, diffusion_in, labels_in, amplitude_in, ctl, dep, scale,
    ext, wext, cext, cown, fix, coef, mid, acc, rim, part, ar, diffusion, labels, amplitude,
    load_sem, halo_send, halo_recv, wind_send, wind_recv,
    root_send, pair_send, pair_recv, hop_send, cross_send, s2_send, sib_send, main_recv,
    edge_send, edge_recv, e2_send, e2_recv, esib_send, esib_recv, ar_send, ar_recv,
):
    fields, levels, rows, cols = ctl.shape
    tall = ext.shape[2]
    regions = amplitude.shape[0]
    m = lax.axis_index("member")
    t = lax.axis_index("tile")
    x, yh, c = m // 4, (m // 2) % 2, m % 2
    mine = 2 * x + c
    sib = m + 1 - 2 * c
    other_half = m + 2 - 4 * yh
    every = range(fields)

    def mate(k):
        return (m + 4 * k) % 16

    def tile(d):
        return (t + d) % TILES

    def remote(src, dst, send, recv, member, at):
        return pltpu.make_async_remote_copy(
            src_ref=src, dst_ref=dst, send_sem=send, recv_sem=recv,
            device_id=(member, at), device_id_type=MESH,
        )

    own = pl.ds(0, rows)
    loads = [
        pltpu.make_async_copy(ens.at[0], ext.at[:, :, own], load_sem.at[0]),
        pltpu.make_async_copy(winds, wext.at[:, :, own], load_sem.at[1]),
        pltpu.make_async_copy(diffusion_in, diffusion, load_sem.at[2]),
        pltpu.make_async_copy(labels_in, labels, load_sem.at[3]),
        pltpu.make_async_copy(amplitude_in, amplitude, load_sem.at[4]),
    ]
    for copy in loads:
        copy.start()
    root_load = pltpu.make_async_copy(ens.at[0], cext, load_sem.at[5])

    @pl.when(m == 0)
    def _():
        root_load.start()

    barrier = pltpu.get_barrier_semaphore()
    near = [mate(1), mate(2), mate(3), sib, other_half, sib + 2 - 4 * yh]
    near += [(sib + 4 * k) % 16 for k in (1, 2, 3)]
    for member in near:
        pl.semaphore_signal(barrier, inc=1, device_id=(member, t), device_id_type=MESH)
    for d in range(1, TILES):
        pl.semaphore_signal(barrier, inc=1, device_id=(m, tile(d)), device_id_type=MESH)
    pl.semaphore_wait(barrier, len(near) + TILES - 1)

    def up(core):
        return [(2, 0), (2 * (1 - core), 1), (1, 0), (1, 1), (1, 2), (0, 0)]

    def down(core):
        return [(2, 2), (2 * core, 1), (3, 0), (3, 1), (3, 2), (0, 2)]

    def plane(f, level):
        return cext.at[f, level]

    def arrival(f, level):
        at = plane(f, level)
        return remote(at, at, hop_send.at[f, level], main_recv.at[f, level], sib, t)

    def pass_on(f, level, member):
        at = plane(f, level)
        return remote(at, at, hop_send.at[f, level], main_recv.at[f, level], member, t)

    def cross(f):
        at = plane(f, mine)
        return remote(at, at, cross_send.at[0, f], main_recv.at[f, mine], other_half, t)

    def to_sib(f, level):
        at = plane(f, level)
        return remote(at, at, sib_send.at[f, level], main_recv.at[f, level], sib, t)

    def root_chain(f, level, member):
        return remote(ens.at[0, f, level], plane(f, level),
                      root_send.at[f, level], main_recv.at[f, level], member, t)

    def root_cross(f, level):
        return remote(ens.at[0, f, level], plane(f, level),
                      cross_send.at[level, f], main_recv.at[f, level], 2 + level, t)

    def root_pair(f):
        return remote(ens.at[0, f], cext.at[f], pair_send.at[f], pair_recv.at[f], 1, t)

    @pl.when(m == 0)
    def _():
        for i in range(6):
            for core in (0, 1):
                q, f = up(core)[i]
                root_chain(f, 2 * q + core, 4 + core).start()
                q, f = down(core)[i]
                root_chain(f, 2 * q + core, 12 + core).start()
            if i < fields:
                for core in (0, 1):
                    root_cross(i, core).start()
        for f in every:
            root_pair(f).start()

    last, first = pl.ds(rows - 2, 2), pl.ds(0, 2)
    low, high = pl.ds(tall - 2, 2), pl.ds(rows, 2)
    wind_last, wind_first = pl.ds(rows - 1, 1), pl.ds(0, 1)
    wind_low, wind_high = pl.ds(tall - 1, 1), pl.ds(rows, 1)
    halos = [
        remote(winds.at[c, :, wind_last], wext.at[c, :, wind_low],
               halo_send.at[2], halo_recv.at[2], m, tile(1)),
        remote(winds.at[c, :, wind_first], wext.at[c, :, wind_high],
               halo_send.at[3], halo_recv.at[3], m, tile(TILES - 1)),
        remote(ens.at[0, :, :, last], ext.at[:, :, low],
               halo_send.at[0], halo_recv.at[0], m, tile(1)),
        remote(ens.at[0, :, :, first], ext.at[:, :, high],
               halo_send.at[1], halo_recv.at[1], m, tile(TILES - 1)),
    ]
    for copy in halos:
        copy.start()

    def level_of(k, core):
        return 2 * ((x + 4 - k) % 4) + core

    def s2(k, f):
        at = plane(f, mine)
        return remote(at, at, s2_send.at[k, f], main_recv.at[f, mine], mate(k), t)

    edges = [
        remote(cext.at[:, mine, last], cown.at[:, low],
               edge_send.at[0], edge_recv.at[0], m, tile(1)),
        remote(cext.at[:, mine, first], cown.at[:, high],
               edge_send.at[1], edge_recv.at[1], m, tile(TILES - 1)),
    ]
    def start_edges():
        for copy in edges:
            copy.start()

    def along(plane_of, member):
        q, f = plane_of
        level = 2 * q + c
        arrival(f, level).wait_recv()
        if member is not None:
            pass_on(f, level, member).start()
        to_sib(f, level).start()

    @pl.when(m == 0)
    def _():
        root_load.wait()
        start_edges()

    @pl.when(m == 1)
    def _():
        for f in every:
            root_pair(f).wait_recv()
        start_edges()

    @pl.when((yh == 0) & (x == 1))
    def _():
        for i, p in enumerate(up(c)):
            along(p, 8 + c)
            if 2 <= i < 5:
                cross(i - 2).start()
            if i == 4:
                start_edges()
        for p in down(c):
            along(p, None)

    @pl.when((yh == 0) & (x == 3))
    def _():
        for i, p in enumerate(down(c)):
            along(p, 8 + c)
            if 2 <= i < 5:
                cross(i - 2).start()
            if i == 4:
                start_edges()
        for p in up(c):
            along(p, None)

    @pl.when((yh == 0) & (x == 2))
    def _():
        for i, (p, n) in enumerate(zip(up(c), down(c))):
            along(p, 12 + c)
            if i == 0:
                cross(0).start()
            along(n, 4 + c)
            if i == 0:
                cross(2).start()
            if i == 1:
                cross(1).start()
                start_edges()

    @pl.when(yh == 1)
    def _():
        for f in every:
            arrival(f, mine).wait_recv()
            for k in (2, 1, 3):
                s2(k, f).start()
            to_sib(f, mine).start()
        start_edges()

    for copy in loads:
        copy.wait()
    wind_pair = [
        remote(wext.at[c, :, at], wext.at[c, :, at], wind_send.at[i], wind_recv.at[i], sib, t)
        for i, at in enumerate((wind_low, wind_high))
    ]
    for copy, pair in zip(halos[:2], wind_pair):
        copy.wait_recv()
        pair.start()
    for i, at in enumerate((wind_low, wind_high)):
        there = wext.at[1 - c, :, at]
        remote(there, there, wind_send.at[i], wind_recv.at[i], sib, t).wait_recv()

    column = lax.broadcasted_iota(jnp.int32, (tall, cols), 1)

    def weigh(level, carry):
        east, north = wext[0, level], wext[1, level]
        k = diffusion[level]
        east_p, east_m = jnp.maximum(east, 0.0), jnp.minimum(east, 0.0)
        north_p, north_m = jnp.maximum(north, 0.0), jnp.minimum(north, 0.0)
        coef[level, 0] = 1.0 - east_p + east_m - north_p + north_m - 4.0 * k
        coef[level, 1] = east_p + k
        coef[level, 2] = k - east_m
        coef[level, 3] = jnp.where(column == 0, 0.0, north_p + k)
        coef[level, 4] = jnp.where(column == cols - 1, 0.0, k - north_m)
        return carry

    lax.fori_loop(0, levels, weigh, 0)

    def step(v, level):
        n = v.shape[0]
        return (
            coef[level, 0, :n] * v
            + coef[level, 1, :n] * pltpu.roll(v, 1, 0)
            + coef[level, 2, :n] * pltpu.roll(v, n - 1, 0)
            + coef[level, 3, :n] * pltpu.roll(v, 1, 1)
            + coef[level, 4, :n] * pltpu.roll(v, cols - 1, 1)
        )

    def two_steps(v, level):
        n = v.shape[0]
        mid[:n] = step(v, level)
        return step(mid[:n], level)[:rows]

    for copy in halos[2:]:
        copy.wait_recv()

    sub = lax.broadcasted_iota(jnp.int32, (8, cols), 0)
    acc[...] = jnp.zeros_like(acc)

    def advance(level, carry):
        for f in every:
            new = two_steps(ext[f, level], level)
            dep[f, level] = new
            rim[f, level] = jnp.where(sub < 4, new[:8], new[8:])
        return carry

    lax.fori_loop(0, levels, advance, 0)

    def gather(f):
        @pl.when(yh == 1)
        def _():
            for k in (1, 3, 2):
                arrival(f, level_of(k, c)).wait_recv()
                to_sib(f, level_of(k, c)).start()

    gather(0)

    def rows_of(ref, level, side):
        if ref is fix:
            return fix.at[:, level, (pl.ds(0, 2), pl.ds(6, 2))[side]]
        return ctl.at[:, level, (first, last)[side]]

    def e2(k, side):
        return remote(rows_of(ctl, mine, side), rows_of(fix, mine, side),
                      e2_send.at[k, side], e2_recv.at[k, side], mate(k), t)

    def e2_in(k, side):
        at = rows_of(fix, level_of(k, c), side)
        return remote(at, at, e2_send.at[k, side], e2_recv.at[k, side], mate(k), t)

    def edge_to_sib(k, side):
        level = level_of(k, c)
        return remote(rows_of(fix if k else ctl, level, side), rows_of(fix, level, side),
                      esib_send.at[k, side], esib_recv.at[k, side], sib, t)

    def edge_from_sib(k, side):
        at = rows_of(fix, level_of(k, 1 - c), side)
        return remote(at, at, esib_send.at[k, side], esib_recv.at[k, side], sib, t)

    for side in (0, 1):
        edges[side].wait_recv()

    def own_level(f, carry):
        cown[f, :rows] = cext[f, mine]
        control = two_steps(cown[f], mine)
        ctl[f, mine] = control
        fix[f, mine] = jnp.where(sub < 4, control[:8], control[8:])
        d = dep[f, mine] - control
        dep[f, mine] = d
        acc[...] = acc[...] + d * d
        return carry

    lax.fori_loop(0, fields, own_level, 0)
    for side in (0, 1):
        for k in (2, 1, 3):
            e2(k, side).start()
        edge_to_sib(0, side).start()

    def other_levels(f):
        @pl.when((yh == 1) | (x > 0))
        def _():
            for k in range(4):
                arrival(f, level_of(k, 1 - c)).wait_recv()

        def one(i, carry):
            level = (mine + 1 + i) % levels
            control = two_steps(cext[f, level], level)
            ctl[f, level] = control
            d = dep[f, level] - control
            dep[f, level] = d
            acc[...] = acc[...] + d * d
            return carry

        lax.fori_loop(0, levels - 1, one, 0)

    gather(1)
    other_levels(0)
    other_levels(1)
    gather(2)
    other_levels(2)

    def blocks(v):
        return sum(v[:, 128 * i:128 * (i + 1)] for i in range(cols // 128))

    def along_lanes(offset):
        sums = jnp.sum(jnp.sum(part[...], axis=1), axis=1, keepdims=True)
        lane = lax.broadcasted_iota(jnp.int32, (regions, 128), 1)
        region = lax.broadcasted_iota(jnp.int32, (regions, 128), 0)
        return jnp.sum(jnp.where(lane == region + offset, sums, 0.0), axis=0, keepdims=True)

    lane = lax.broadcasted_iota(jnp.int32, (1, 128), 1)
    target = jnp.zeros((1, 128), jnp.float32)
    outer = (sub < 2) | (sub >= 6)
    where_label = labels[...]
    for r in range(regions):
        one = (where_label == r).astype(jnp.float32)
        part[r] = blocks(one[:8] + one[8:])
        target = jnp.where(lane == r, amplitude[r], target)
    counts = along_lanes(regions)
    top = jnp.where(sub < 2, 0.0, acc[:8])
    bottom = jnp.where(sub >= 6, 0.0, acc[8:])
    for r in range(regions):
        part[r] = blocks(
            jnp.where(where_label[:8] == r, top, 0.0) + jnp.where(where_label[8:] == r, bottom, 0.0)
        )

    def depart(level, total):
        for f in every:
            d = rim[f, level] - fix[f, level]
            total = total + d * d
        return total

    total = depart(mine, jnp.zeros((8, cols), jnp.float32))
    for k in (1, 3, 2):
        for side in (0, 1):
            e2_in(k, side).wait_recv()
            edge_to_sib(k, side).start()
        total = depart(level_of(k, c), total)
    for k in (0, 1, 3, 2):
        for side in (0, 1):
            edge_from_sib(k, side).wait_recv()
        total = depart(level_of(k, 1 - c), total)
    label_rim = jnp.where(sub < 4, where_label[:8], where_label[8:])
    label_rim = jnp.where(outer, label_rim, -1)
    for r in range(regions):
        part[r] = part[r] + blocks(jnp.where(label_rim == r, total, 0.0))
    ar[0] = along_lanes(0) + counts

    def ar_copy(d):
        return remote(ar.at[0], ar.at[d], ar_send, ar_recv, m, tile(d))

    far_first = sorted(range(1, TILES), key=lambda d: abs(d - TILES // 2))
    for d in far_first:
        ar_copy(d).start()

    def patch(i, carry):
        level = (mine + 1 + i) % levels
        for f in every:
            edge = fix[f, level]
            d = rim[f, level] - edge
            ctl[f, level, :8] = jnp.where(sub < 2, edge, ctl[f, level, :8])
            ctl[f, level, 8:] = jnp.where(sub >= 6, edge, ctl[f, level, 8:])
            dep[f, level, :8] = jnp.where(sub < 2, d, dep[f, level, :8])
            dep[f, level, 8:] = jnp.where(sub >= 6, d, dep[f, level, 8:])
        return carry

    lax.fori_loop(0, levels - 1, patch, 0)
    rest = ar.at[pl.ds(1, TILES - 1)]
    pltpu.make_async_copy(rest, rest, ar_recv).wait()
    total = jnp.sum(ar[...], axis=0)
    counts = pltpu.roll(total, 128 - regions, 1)
    counts = jnp.where(lane < regions, counts, 1.0)
    factor = target / jnp.sqrt(total / (counts * (fields * levels)) + 1e-06)
    scales = jnp.zeros((rows, cols), jnp.float32)
    for r in range(regions):
        scales = jnp.where(where_label == r, factor[:, r:r + 1], scales)
    scale[...] = scales

    pltpu.make_async_copy(rest, rest, ar_send).wait()
    for copy in halos + edges + wind_pair:
        copy.wait_send()

    @pl.when(m == 0)
    def _():
        for f in every:
            for level in range(levels):
                root_chain(f, level, 4).wait_send()
            for core in (0, 1):
                root_cross(f, core).wait_send()
            root_pair(f).wait_send()

    @pl.when((yh == 1) | (x > 0))
    def _():
        for f in every:
            for k in range(4):
                to_sib(f, 2 * k + c).wait_send()

    @pl.when((yh == 0) & (x > 0))
    def _():
        for f in every:
            cross(f).wait_send()

    @pl.when((yh == 0) & ((x == 1) | (x == 2)))
    def _():
        for q, f in up(c):
            pass_on(f, 2 * q + c, sib).wait_send()

    @pl.when((yh == 0) & ((x == 3) | (x == 2)))
    def _():
        for q, f in down(c):
            pass_on(f, 2 * q + c, sib).wait_send()

    @pl.when(yh == 1)
    def _():
        for f in every:
            for k in (1, 2, 3):
                s2(k, f).wait_send()

    for side in (0, 1):
        for k in (1, 2, 3):
            e2(k, side).wait_send()
        for k in range(4):
            edge_to_sib(k, side).wait_send()


def on_device(ensemble, winds, diffusion, labels, amplitude):
    _, fields, levels, rows, cols = ensemble.shape
    block = jax.ShapeDtypeStruct((fields, levels, rows, cols), jnp.float32)
    f32 = jnp.float32
    tall = rows + 8
    vmem = pl.BlockSpec(memory_space=pltpu.VMEM)
    hbm = pl.BlockSpec(memory_space=pltpu.HBM)
    inputs = [
        pltpu.with_memory_space_constraint(a, pltpu.HBM)
        for a in (ensemble, winds, diffusion, labels, amplitude)
    ]
    pair = (DMA((4, 2)), DMA((4, 2)))
    planes = DMA((fields, levels))
    control, departure, scale = pl.pallas_call(
        kernel,
        name="breed",
        out_shape=(block, block, jax.ShapeDtypeStruct((rows, cols), f32)),
        in_specs=[hbm] * 5,
        out_specs=(vmem, vmem, vmem),
        scratch_shapes=[
            pltpu.VMEM((fields, levels, tall, cols), f32),
            pltpu.VMEM((2, levels, tall, cols), f32),
            pltpu.VMEM((fields, levels, rows, cols), f32),
            pltpu.VMEM((fields, tall, cols), f32),
            pltpu.VMEM((fields, levels, 8, cols), f32),
            pltpu.VMEM((levels, 5, tall, cols), f32),
            pltpu.VMEM((tall, cols), f32),
            pltpu.VMEM((rows, cols), f32),
            pltpu.VMEM((fields, levels, 8, cols), f32),
            pltpu.VMEM((amplitude.shape[0], 8, 128), f32),
            pltpu.VMEM((TILES, 1, 128), f32),
            pltpu.SMEM((levels,), f32),
            pltpu.VMEM((rows, cols), jnp.int32),
            pltpu.SMEM(amplitude.shape, f32),
            DMA((6,)), DMA((4,)), DMA((4,)), DMA((2,)), DMA((2,)),
            planes, DMA((fields,)), DMA((fields,)), planes, DMA((2, fields)),
            DMA((4, fields)), planes, planes,
            DMA((2,)), DMA((2,)), *pair, *pair, DMA, DMA,
        ],
        compiler_params=pltpu.CompilerParams(
            collective_id=0, has_side_effects=True, vmem_limit_bytes=32 * 2**20
        ),
    )(*inputs)
    return (control + departure * scale)[None]


def solution(mesh):
    return jax.shard_map(
        on_device,
        mesh=mesh,
        in_specs=(
            P("member", None, None, "tile", None),
            P(None, None, "tile", None),
            P(),
            P("tile", None),
            P(),
        ),
        out_specs=P("member", None, None, "tile", None),
        check_vma=False,
    )
```

```python
import jax
import jax.numpy as jnp
from jax import lax
from jax.experimental import pallas as pl
from jax.experimental.pallas import tpu as pltpu
from jax.sharding import PartitionSpec as P

MESH = pl.DeviceIdType.MESH
DMA = pltpu.SemaphoreType.DMA
TILES = 32


def kernel(
    ens, winds, diffusion_in, labels_in, amplitude_in, ctl, dep, scale,
    ext, wext, cext, cown, fix, coef, mid, acc, rim, part, ar, diffusion, labels, amplitude,
    load_sem, halo_send, halo_recv, wind_send, wind_recv,
    root_send, pair_send, pair_recv, hop_send, cross_send, s2_send, sib_send, main_recv,
    edge_send, edge_recv, e2_send, e2_recv, esib_send, esib_recv, ar_send, ar_recv,
):
    fields, levels, rows, cols = ctl.shape
    tall = ext.shape[2]
    regions = amplitude.shape[0]
    m = lax.axis_index("member")
    t = lax.axis_index("tile")
    x, yh, c = m // 4, (m // 2) % 2, m % 2
    mine = 2 * x + c
    sib = m + 1 - 2 * c
    other_half = m + 2 - 4 * yh
    every = range(fields)

    def mate(k):
        return (m + 4 * k) % 16

    def tile(d):
        return (t + d) % TILES

    def remote(src, dst, send, recv, member, at):
        return pltpu.make_async_remote_copy(
            src_ref=src, dst_ref=dst, send_sem=send, recv_sem=recv,
            device_id=(member, at), device_id_type=MESH,
        )

    own = pl.ds(0, rows)
    loads = [
        pltpu.make_async_copy(ens.at[0], ext.at[:, :, own], load_sem.at[0]),
        pltpu.make_async_copy(winds, wext.at[:, :, own], load_sem.at[1]),
        pltpu.make_async_copy(diffusion_in, diffusion, load_sem.at[2]),
        pltpu.make_async_copy(labels_in, labels, load_sem.at[3]),
        pltpu.make_async_copy(amplitude_in, amplitude, load_sem.at[4]),
    ]
    for copy in loads:
        copy.start()
    root_load = pltpu.make_async_copy(ens.at[0], cext, load_sem.at[5])

    @pl.when(m == 0)
    def _():
        root_load.start()

    barrier = pltpu.get_barrier_semaphore()
    near = [mate(1), mate(2), mate(3), sib, other_half, sib + 2 - 4 * yh]
    near += [(sib + 4 * k) % 16 for k in (1, 2, 3)]
    for member in near:
        pl.semaphore_signal(barrier, inc=1, device_id=(member, t), device_id_type=MESH)
    for d in range(1, TILES):
        pl.semaphore_signal(barrier, inc=1, device_id=(m, tile(d)), device_id_type=MESH)
    pl.semaphore_wait(barrier, len(near) + TILES - 1)

    def up(core):
        return [(2, 0), (2 * (1 - core), 1), (1, 0), (1, 1), (1, 2), (0, 0)]

    def down(core):
        return [(2, 2), (2 * core, 1), (3, 0), (3, 1), (3, 2), (0, 2)]

    def plane(f, level):
        return cext.at[f, level]

    def arrival(f, level):
        at = plane(f, level)
        return remote(at, at, hop_send.at[f, level], main_recv.at[f, level], sib, t)

    def pass_on(f, level, member):
        at = plane(f, level)
        return remote(at, at, hop_send.at[f, level], main_recv.at[f, level], member, t)

    def cross(f):
        at = plane(f, mine)
        return remote(at, at, cross_send.at[0, f], main_recv.at[f, mine], other_half, t)

    def to_sib(f, level):
        at = plane(f, level)
        return remote(at, at, sib_send.at[f, level], main_recv.at[f, level], sib, t)

    def root_chain(f, level, member):
        return remote(ens.at[0, f, level], plane(f, level),
                      root_send.at[f, level], main_recv.at[f, level], member, t)

    def root_cross(f, level):
        return remote(ens.at[0, f, level], plane(f, level),
                      cross_send.at[level, f], main_recv.at[f, level], 2 + level, t)

    def root_pair(f):
        return remote(ens.at[0, f], cext.at[f], pair_send.at[f], pair_recv.at[f], 1, t)

    @pl.when(m == 0)
    def _():
        for i in range(6):
            for core in (0, 1):
                q, f = up(core)[i]
                root_chain(f, 2 * q + core, 4 + core).start()
                q, f = down(core)[i]
                root_chain(f, 2 * q + core, 12 + core).start()
            if i < fields:
                for core in (0, 1):
                    root_cross(i, core).start()
        for f in every:
            root_pair(f).start()

    last, first = pl.ds(rows - 2, 2), pl.ds(0, 2)
    low, high = pl.ds(tall - 2, 2), pl.ds(rows, 2)
    wind_last, wind_first = pl.ds(rows - 1, 1), pl.ds(0, 1)
    wind_low, wind_high = pl.ds(tall - 1, 1), pl.ds(rows, 1)
    halos = [
        remote(winds.at[c, :, wind_last], wext.at[c, :, wind_low],
               halo_send.at[2], halo_recv.at[2], m, tile(1)),
        remote(winds.at[c, :, wind_first], wext.at[c, :, wind_high],
               halo_send.at[3], halo_recv.at[3], m, tile(TILES - 1)),
        remote(ens.at[0, :, :, last], ext.at[:, :, low],
               halo_send.at[0], halo_recv.at[0], m, tile(1)),
        remote(ens.at[0, :, :, first], ext.at[:, :, high],
               halo_send.at[1], halo_recv.at[1], m, tile(TILES - 1)),
    ]
    for copy in halos:
        copy.start()

    def level_of(k, core):
        return 2 * ((x + 4 - k) % 4) + core

    def s2(k, f):
        at = plane(f, mine)
        return remote(at, at, s2_send.at[k, f], main_recv.at[f, mine], mate(k), t)

    edges = [
        remote(cext.at[:, mine, last], cown.at[:, low],
               edge_send.at[0], edge_recv.at[0], m, tile(1)),
        remote(cext.at[:, mine, first], cown.at[:, high],
               edge_send.at[1], edge_recv.at[1], m, tile(TILES - 1)),
    ]
    def start_edges():
        for copy in edges:
            copy.start()

    def along(plane_of, member):
        q, f = plane_of
        level = 2 * q + c
        arrival(f, level).wait_recv()
        if member is not None:
            pass_on(f, level, member).start()
        to_sib(f, level).start()

    @pl.when(m == 0)
    def _():
        root_load.wait()
        start_edges()

    @pl.when(m == 1)
    def _():
        for f in every:
            root_pair(f).wait_recv()
        start_edges()

    @pl.when((yh == 0) & (x == 1))
    def _():
        for i, p in enumerate(up(c)):
            along(p, 8 + c)
            if 2 <= i < 5:
                cross(i - 2).start()
            if i == 4:
                start_edges()
        for p in down(c):
            along(p, None)

    @pl.when((yh == 0) & (x == 3))
    def _():
        for i, p in enumerate(down(c)):
            along(p, 8 + c)
            if 2 <= i < 5:
                cross(i - 2).start()
            if i == 4:
                start_edges()
        for p in up(c):
            along(p, None)

    @pl.when((yh == 0) & (x == 2))
    def _():
        for i, (p, n) in enumerate(zip(up(c), down(c))):
            along(p, 12 + c)
            if i == 0:
                cross(0).start()
            along(n, 4 + c)
            if i == 0:
                cross(2).start()
            if i == 1:
                cross(1).start()
                start_edges()

    @pl.when(yh == 1)
    def _():
        for f in every:
            arrival(f, mine).wait_recv()
            for k in (2, 1, 3):
                s2(k, f).start()
            to_sib(f, mine).start()
        start_edges()

    for copy in loads:
        copy.wait()
    wind_pair = [
        remote(wext.at[c, :, at], wext.at[c, :, at], wind_send.at[i], wind_recv.at[i], sib, t)
        for i, at in enumerate((wind_low, wind_high))
    ]
    for copy, pair in zip(halos[:2], wind_pair):
        copy.wait_recv()
        pair.start()
    for i, at in enumerate((wind_low, wind_high)):
        there = wext.at[1 - c, :, at]
        remote(there, there, wind_send.at[i], wind_recv.at[i], sib, t).wait_recv()

    column = lax.broadcasted_iota(jnp.int32, (tall, cols), 1)

    def weigh(level, carry):
        east, north = wext[0, level], wext[1, level]
        k = diffusion[level]
        east_p, east_m = jnp.maximum(east, 0.0), jnp.minimum(east, 0.0)
        north_p, north_m = jnp.maximum(north, 0.0), jnp.minimum(north, 0.0)
        coef[level, 0] = 1.0 - east_p + east_m - north_p + north_m - 4.0 * k
        coef[level, 1] = east_p + k
        coef[level, 2] = k - east_m
        coef[level, 3] = jnp.where(column == 0, 0.0, north_p + k)
        coef[level, 4] = jnp.where(column == cols - 1, 0.0, k - north_m)
        return carry

    lax.fori_loop(0, levels, weigh, 0)

    def step(v, level):
        n = v.shape[0]
        return (
            coef[level, 0, :n] * v
            + coef[level, 1, :n] * pltpu.roll(v, 1, 0)
            + coef[level, 2, :n] * pltpu.roll(v, n - 1, 0)
            + coef[level, 3, :n] * pltpu.roll(v, 1, 1)
            + coef[level, 4, :n] * pltpu.roll(v, cols - 1, 1)
        )

    def two_steps(v, level):
        n = v.shape[0]
        mid[:n] = step(v, level)
        return step(mid[:n], level)[:rows]

    for copy in halos[2:]:
        copy.wait_recv()

    sub = lax.broadcasted_iota(jnp.int32, (8, cols), 0)
    acc[...] = jnp.zeros_like(acc)

    def advance(level, carry):
        for f in every:
            new = two_steps(ext[f, level], level)
            dep[f, level] = new
            rim[f, level] = jnp.where(sub < 4, new[:8], new[8:])
        return carry

    lax.fori_loop(0, levels, advance, 0)

    def gather(f):
        @pl.when(yh == 1)
        def _():
            for k in (1, 3, 2):
                arrival(f, level_of(k, c)).wait_recv()
                to_sib(f, level_of(k, c)).start()

    gather(0)

    def rows_of(ref, level, side):
        if ref is fix:
            return fix.at[:, level, (pl.ds(0, 2), pl.ds(6, 2))[side]]
        return ctl.at[:, level, (first, last)[side]]

    def e2(k, side):
        return remote(rows_of(ctl, mine, side), rows_of(fix, mine, side),
                      e2_send.at[k, side], e2_recv.at[k, side], mate(k), t)

    def e2_in(k, side):
        at = rows_of(fix, level_of(k, c), side)
        return remote(at, at, e2_send.at[k, side], e2_recv.at[k, side], mate(k), t)

    def edge_to_sib(k, side):
        level = level_of(k, c)
        return remote(rows_of(fix if k else ctl, level, side), rows_of(fix, level, side),
                      esib_send.at[k, side], esib_recv.at[k, side], sib, t)

    def edge_from_sib(k, side):
        at = rows_of(fix, level_of(k, 1 - c), side)
        return remote(at, at, esib_send.at[k, side], esib_recv.at[k, side], sib, t)

    for side in (0, 1):
        edges[side].wait_recv()

    def own_level(f, carry):
        cown[f, :rows] = cext[f, mine]
        control = two_steps(cown[f], mine)
        ctl[f, mine] = control
        fix[f, mine] = jnp.where(sub < 4, control[:8], control[8:])
        d = dep[f, mine] - control
        dep[f, mine] = d
        acc[...] = acc[...] + d * d
        return carry

    lax.fori_loop(0, fields, own_level, 0)
    for side in (0, 1):
        for k in (2, 1, 3):
            e2(k, side).start()
        edge_to_sib(0, side).start()

    def other_levels(f):
        @pl.when((yh == 1) | (x > 0))
        def _():
            for k in range(4):
                arrival(f, level_of(k, 1 - c)).wait_recv()

        def one(i, carry):
            level = (mine + 1 + i) % levels
            control = two_steps(cext[f, level], level)
            ctl[f, level] = control
            d = dep[f, level] - control
            dep[f, level] = d
            acc[...] = acc[...] + d * d
            return carry

        lax.fori_loop(0, levels - 1, one, 0)

    gather(1)
    gather(2)
    other_levels(0)
    other_levels(1)
    other_levels(2)

    def blocks(v):
        return sum(v[:, 128 * i:128 * (i + 1)] for i in range(cols // 128))

    def along_lanes(offset):
        sums = jnp.sum(jnp.sum(part[...], axis=1), axis=1, keepdims=True)
        lane = lax.broadcasted_iota(jnp.int32, (regions, 128), 1)
        region = lax.broadcasted_iota(jnp.int32, (regions, 128), 0)
        return jnp.sum(jnp.where(lane == region + offset, sums, 0.0), axis=0, keepdims=True)

    lane = lax.broadcasted_iota(jnp.int32, (1, 128), 1)
    target = jnp.zeros((1, 128), jnp.float32)
    outer = (sub < 2) | (sub >= 6)
    where_label = labels[...]
    for r in range(regions):
        one = (where_label == r).astype(jnp.float32)
        part[r] = blocks(one[:8] + one[8:])
        target = jnp.where(lane == r, amplitude[r], target)
    counts = along_lanes(regions)
    top = jnp.where(sub < 2, 0.0, acc[:8])
    bottom = jnp.where(sub >= 6, 0.0, acc[8:])
    for r in range(regions):
        part[r] = blocks(
            jnp.where(where_label[:8] == r, top, 0.0) + jnp.where(where_label[8:] == r, bottom, 0.0)
        )

    def depart(level, total):
        for f in every:
            d = rim[f, level] - fix[f, level]
            total = total + d * d
        return total

    total = depart(mine, jnp.zeros((8, cols), jnp.float32))
    for k in (1, 3, 2):
        for side in (0, 1):
            e2_in(k, side).wait_recv()
            edge_to_sib(k, side).start()
        total = depart(level_of(k, c), total)
    for k in (0, 1, 3, 2):
        for side in (0, 1):
            edge_from_sib(k, side).wait_recv()
        total = depart(level_of(k, 1 - c), total)
    label_rim = jnp.where(sub < 4, where_label[:8], where_label[8:])
    label_rim = jnp.where(outer, label_rim, -1)
    for r in range(regions):
        part[r] = part[r] + blocks(jnp.where(label_rim == r, total, 0.0))
    ar[0] = along_lanes(0) + counts

    def ar_copy(d):
        return remote(ar.at[0], ar.at[d], ar_send, ar_recv, m, tile(d))

    far_first = sorted(range(1, TILES), key=lambda d: abs(d - TILES // 2))
    for d in far_first:
        ar_copy(d).start()

    def patch(i, carry):
        level = (mine + 1 + i) % levels
        for f in every:
            edge = fix[f, level]
            d = rim[f, level] - edge
            ctl[f, level, :8] = jnp.where(sub < 2, edge, ctl[f, level, :8])
            ctl[f, level, 8:] = jnp.where(sub >= 6, edge, ctl[f, level, 8:])
            dep[f, level, :8] = jnp.where(sub < 2, d, dep[f, level, :8])
            dep[f, level, 8:] = jnp.where(sub >= 6, d, dep[f, level, 8:])
        return carry

    lax.fori_loop(0, levels - 1, patch, 0)
    rest = ar.at[pl.ds(1, TILES - 1)]
    pltpu.make_async_copy(rest, rest, ar_recv).wait()
    total = jnp.sum(ar[...], axis=0)
    counts = pltpu.roll(total, 128 - regions, 1)
    counts = jnp.where(lane < regions, counts, 1.0)
    factor = target / jnp.sqrt(total / (counts * (fields * levels)) + 1e-06)
    scales = jnp.zeros((rows, cols), jnp.float32)
    for r in range(regions):
        scales = jnp.where(where_label == r, factor[:, r:r + 1], scales)
    scale[...] = scales

    pltpu.make_async_copy(rest, rest, ar_send).wait()
    for copy in halos + edges + wind_pair:
        copy.wait_send()

    @pl.when(m == 0)
    def _():
        for f in every:
            for level in range(levels):
                root_chain(f, level, 4).wait_send()
            for core in (0, 1):
                root_cross(f, core).wait_send()
            root_pair(f).wait_send()

    @pl.when((yh == 1) | (x > 0))
    def _():
        for f in every:
            for k in range(4):
                to_sib(f, 2 * k + c).wait_send()

    @pl.when((yh == 0) & (x > 0))
    def _():
        for f in every:
            cross(f).wait_send()

    @pl.when((yh == 0) & ((x == 1) | (x == 2)))
    def _():
        for q, f in up(c):
            pass_on(f, 2 * q + c, sib).wait_send()

    @pl.when((yh == 0) & ((x == 3) | (x == 2)))
    def _():
        for q, f in down(c):
            pass_on(f, 2 * q + c, sib).wait_send()

    @pl.when(yh == 1)
    def _():
        for f in every:
            for k in (1, 2, 3):
                s2(k, f).wait_send()

    for side in (0, 1):
        for k in (1, 2, 3):
            e2(k, side).wait_send()
        for k in range(4):
            edge_to_sib(k, side).wait_send()


def on_device(ensemble, winds, diffusion, labels, amplitude):
    _, fields, levels, rows, cols = ensemble.shape
    block = jax.ShapeDtypeStruct((fields, levels, rows, cols), jnp.float32)
    f32 = jnp.float32
    tall = rows + 8
    vmem = pl.BlockSpec(memory_space=pltpu.VMEM)
    hbm = pl.BlockSpec(memory_space=pltpu.HBM)
    inputs = [
        pltpu.with_memory_space_constraint(a, pltpu.HBM)
        for a in (ensemble, winds, diffusion, labels, amplitude)
    ]
    pair = (DMA((4, 2)), DMA((4, 2)))
    planes = DMA((fields, levels))
    control, departure, scale = pl.pallas_call(
        kernel,
        name="breed",
        out_shape=(block, block, jax.ShapeDtypeStruct((rows, cols), f32)),
        in_specs=[hbm] * 5,
        out_specs=(vmem, vmem, vmem),
        scratch_shapes=[
            pltpu.VMEM((fields, levels, tall, cols), f32),
            pltpu.VMEM((2, levels, tall, cols), f32),
            pltpu.VMEM((fields, levels, rows, cols), f32),
            pltpu.VMEM((fields, tall, cols), f32),
            pltpu.VMEM((fields, levels, 8, cols), f32),
            pltpu.VMEM((levels, 5, tall, cols), f32),
            pltpu.VMEM((tall, cols), f32),
            pltpu.VMEM((rows, cols), f32),
            pltpu.VMEM((fields, levels, 8, cols), f32),
            pltpu.VMEM((amplitude.shape[0], 8, 128), f32),
            pltpu.VMEM((TILES, 1, 128), f32),
            pltpu.SMEM((levels,), f32),
            pltpu.VMEM((rows, cols), jnp.int32),
            pltpu.SMEM(amplitude.shape, f32),
            DMA((6,)), DMA((4,)), DMA((4,)), DMA((2,)), DMA((2,)),
            planes, DMA((fields,)), DMA((fields,)), planes, DMA((2, fields)),
            DMA((4, fields)), planes, planes,
            DMA((2,)), DMA((2,)), *pair, *pair, DMA, DMA,
        ],
        compiler_params=pltpu.CompilerParams(
            collective_id=0, has_side_effects=True, vmem_limit_bytes=32 * 2**20
        ),
    )(*inputs)
    return (control + departure * scale)[None]


def solution(mesh):
    return jax.shard_map(
        on_device,
        mesh=mesh,
        in_specs=(
            P("member", None, None, "tile", None),
            P(None, None, "tile", None),
            P(),
            P("tile", None),
            P(),
        ),
        out_specs=P("member", None, None, "tile", None),
        check_vma=False,
    )
```
